512 devices in a mesh: dp: 512 (over y, x, z, core).
Axes of the slice: x: 4, y: 4, z: 16, core: 2. Of those that a mesh axis runs over, the one named last changes fastest.
Arguments:
- picture_encoder_result: float32 [131072, 1152], P('dp'), may hold values from -0.1875 to 0.1875
- caption_encoder_result: float32 [131072, 1152], P('dp'), may hold values from -0.1875 to 0.1875
- picture_channel_factor: float32 [1152], replicated, may hold values from 0.25 to 1.75
- caption_channel_factor: float32 [1152], replicated, may hold values from 0.25 to 1.75
- logit_multiplier: float32 [], replicated, may hold values from 5 to 15
- logit_offset: float32 [], replicated, may hold values from -4 to -1
Outputs:
- image_grad: float32 [131072, 1152], P('dp')
- text_grad: float32 [131072, 1152], P('dp')
- image_gain_grad: float32 [1152], replicated
- text_gain_grad: float32 [1152], replicated
- temp_grad: float32 [], replicated
- bias_grad: float32 [], replicated
- loss: float32 [], replicated
The draws below stay inside these ranges and needn't reach their ends.
All inputs are finite; a program needn't handle non-finite values.
Results may differ from the reference program's by a relative error of at most 0.00012.
Values sent between devices are 32-bit elements; how exact they have to be, the bound alone decides.
A program may use at most 64 MiB of HBM per device.

```python
import jax
import jax.numpy as jnp
from jax import lax

D = 1152
ROWS = 256
TOKENS = 131072
PAIRS = 100663296
N_DP = 512


def block_levels(key, extent, split, smallest, high):
    def one(dim, parts):
        draws = jax.random.uniform(jax.random.fold_in(jax.random.fold_in(key, 6), dim), (parts,), jnp.float32, smallest / len(split), high / len(split))
        return jnp.repeat(jnp.exp(draws), extent[dim] // parts).reshape((-1,) + (1,) * (len(extent) - dim - 1))

    level = one(*split[0])
    for cut in split[1:]:
        level = level * one(*cut)
    return level


def normal_values(key, shape, deviation, limit, shards=(), kind=jnp.bfloat16):
    drawn = deviation * jax.random.normal(key, shape, jnp.float32)
    if shards:
        drawn = drawn * block_levels(key, shape, shards, -0.22, 0.18)
    return jnp.clip(drawn, -limit, limit).astype(kind)


def setup_inputs(seed: int = 0) -> dict:
    keys = jax.random.split(jax.random.key(seed), 7)
    return {
        "picture_encoder_result": normal_values(keys[0], (TOKENS, D), D ** -0.5, 0.1875, ((0, 512),), jnp.float32),
        "caption_encoder_result": normal_values(keys[1], (TOKENS, D), D ** -0.5, 0.1875, ((0, 512),), jnp.float32),
        "picture_channel_factor": jnp.clip(1.0 + 0.15 * jax.random.normal(keys[2], (D,), jnp.float32), 0.25, 1.75),
        "caption_channel_factor": jnp.clip(1.0 + 0.15 * jax.random.normal(keys[3], (D,), jnp.float32), 0.25, 1.75),
        "logit_multiplier": jnp.clip(jax.random.uniform(keys[4], (), jnp.float32, 5.0, 15.0), 5.0, 15.0),
        "logit_offset": jnp.clip(jax.random.uniform(keys[5], (), jnp.float32, -4.0, -1.0), -4.0, -1.0),
    }


eps = 1e-06

def normalize(feat, gain):
    scaled = feat * gain
    norm = jnp.sqrt(lax.optimization_barrier(jnp.sum(scaled * scaled, axis=-1, keepdims=True)) + eps)
    return (scaled / norm, norm)

def partner_round_loop(picture_unit_rows, caption_unit_rows, logit_multiplier, logit_offset, resident_slice):
    round_update = jnp.dot(picture_unit_rows, caption_unit_rows.T, precision=lax.Precision.HIGHEST, preferred_element_type=jnp.float32)
    match_logit_matrix = logit_multiplier * round_update + logit_offset
    labels = resident_slice * jnp.eye(picture_unit_rows.shape[0], dtype=jnp.float32)
    pair_loss = jnp.sum(jax.nn.softplus(match_logit_matrix) - labels * match_logit_matrix)
    derivative_collection = jax.nn.sigmoid(match_logit_matrix) - labels
    picture_vector_derivative = logit_multiplier * jnp.dot(derivative_collection, caption_unit_rows, precision=lax.Precision.HIGHEST, preferred_element_type=jnp.float32)
    caption_vector_derivative = logit_multiplier * jnp.dot(derivative_collection.T, picture_unit_rows, precision=lax.Precision.HIGHEST, preferred_element_type=jnp.float32)
    return (picture_vector_derivative, caption_vector_derivative, pair_loss, jnp.sum(derivative_collection * round_update), jnp.sum(derivative_collection))

def backward_norm(d_emb, emb, norm, feat, gain):
    d_scaled = (d_emb - emb * lax.optimization_barrier(jnp.sum(emb * d_emb, axis=-1, keepdims=True))) / norm
    return (d_scaled * gain, lax.optimization_barrier(jnp.sum(d_scaled * feat, axis=0)))

def reference(picture_encoder_result, caption_encoder_result, picture_channel_factor, caption_channel_factor, logit_multiplier, logit_offset):
    picture_unit_rows, image_norm = normalize(picture_encoder_result, picture_channel_factor)
    caption_unit_rows, text_norm = normalize(caption_encoder_result, caption_channel_factor)
    log_dev = N_DP.bit_length() - 1
    far = log_dev - 1
    near = log_dev // 2
    image_blocks = picture_unit_rows.reshape(N_DP, ROWS, D)
    text_blocks = caption_unit_rows.reshape(N_DP, ROWS, D)
    index = jnp.arange(N_DP, dtype=jnp.int32)
    picture_vector_derivative = jnp.zeros_like(image_blocks)
    caption_vector_derivative = jnp.zeros_like(text_blocks)
    totals = jnp.zeros((3,), jnp.float32)
    for offset in (0, 1 << far, 1 << near):
        perm = jnp.bitwise_xor(index, offset).astype(jnp.int32)
        partner = text_blocks[perm]
        resident_slice = 1.0 if offset == 0 else 0.0

        def one_block(match_logit):
            return partner_round_loop(match_logit[0], match_logit[1], logit_multiplier, logit_offset, resident_slice)
        d_img, d_txt, losses, temps, biases = lax.map(one_block, (image_blocks, partner))
        picture_vector_derivative = picture_vector_derivative + d_img
        caption_vector_derivative = caption_vector_derivative + d_txt[perm]
        totals = totals + jnp.stack([jnp.sum(losses), jnp.sum(temps), jnp.sum(biases)])
    image_grad, image_gain_grad = backward_norm(picture_vector_derivative.reshape(TOKENS, D), picture_unit_rows, image_norm, picture_encoder_result, picture_channel_factor)
    text_grad, text_gain_grad = backward_norm(caption_vector_derivative.reshape(TOKENS, D), caption_unit_rows, text_norm, caption_encoder_result, caption_channel_factor)
    return (image_grad, text_grad, image_gain_grad, text_gain_grad, totals[1] / PAIRS, totals[2] / PAIRS, totals[0] / PAIRS)
```

```python
import functools

import jax
import jax.numpy as jnp
from jax import lax
from jax.experimental import pallas as pl
from jax.experimental.pallas import tpu as pltpu
from jax.sharding import PartitionSpec as P

eps = 1e-06
MESH = pl.DeviceIdType.MESH

ROWS = 256
D = 1152
CHUNKS = 2
CHUNK = ROWS // CHUNKS
HALF = CHUNK // 2
Z = 16
HOPS = Z // 2
BITS = 9
FAR_BIT = 8
NEAR_BIT = 4
SUM_BITS = (0, 5, 6, 7, 8, 1, 2, 3, 4)
LANES = 128
TILES = D // LANES
PAY = 24
SELF, FAR, NEAR = 0, 1, 2


def flipped(me, bit):
    stride = 1 << bit
    return me + stride - 2 * stride * ((me // stride) % 2)


def z_shifted(me, step):
    z = (me // 2) % Z
    return me + 2 * ((z + step + Z) % Z - z)


def matmul(a, b, contract):
    return lax.dot_general(
        a,
        b,
        ((contract[:1], contract[1:]), ((), ())),
        precision=lax.Precision.HIGHEST,
        preferred_element_type=jnp.float32,
    )


def kernel(
    mult_ref,
    offs_ref,
    img_hbm,
    txt_hbm,
    gi_ref,
    gt_ref,
    img_grad_ref,
    txt_grad_ref,
    img_gain_ref,
    txt_gain_ref,
    sums_ref,
    img_raw,
    txt_raw,
    img_emb,
    d_img,
    hops,
    ret,
    far_in,
    far_ret,
    far_back,
    g_all,
    e_all,
    gain_acc,
    sum_acc,
    pay,
    pay_in,
    load_sem,
    send_sem,
    recv_sem,
    far_send,
    far_recv,
    pay_send,
    pay_recv,
):
    me = lax.axis_index("dp")
    ways = (z_shifted(me, 1), z_shifted(me, -1))
    far = flipped(me, FAR_BIT)
    mult = mult_ref[0]
    offs = offs_ref[0]

    barrier = pltpu.get_barrier_semaphore()
    for other in ways + tuple(flipped(me, bit) for bit in range(BITS)):
        pl.semaphore_signal(barrier, inc=1, device_id=(other,), device_id_type=MESH)
    pl.semaphore_wait(barrier, BITS + 2)

    def hop(phase, h, k, d, src):
        return pltpu.make_async_remote_copy(
            src_ref=src,
            dst_ref=hops.at[phase, h, k, pl.ds(d * HALF, HALF)],
            send_sem=send_sem.at[phase, h, k, d],
            recv_sem=recv_sem.at[phase, h, k, d],
            device_id=(ways[d],),
            device_id_type=MESH,
        )

    def landed(phase, h, k, d):
        return hops.at[phase, h, k, pl.ds(d * HALF, HALF)]

    def forward(phase, h, k):
        for d in range(2):
            src = landed(phase, h, k, d)
            hop(phase, h, k, d, src).wait_recv()
            hop(phase, h + 1, k, d, src).start()

    def sent(phase, h, k):
        for d in range(2):
            hop(phase, h, k, d, landed(phase, h, k, d)).wait_send()

    def far_copy(leg, k, src, dst):
        return pltpu.make_async_remote_copy(
            src_ref=src.at[pl.ds(k * CHUNK, CHUNK)],
            dst_ref=dst.at[pl.ds(k * CHUNK, CHUNK)],
            send_sem=far_send.at[leg, k],
            recv_sem=far_recv.at[leg, k],
            device_id=(far,),
            device_id_type=MESH,
        )

    def pay_copy(step):
        return pltpu.make_async_remote_copy(
            src_ref=pay.at[step],
            dst_ref=pay_in.at[step],
            send_sem=pay_send.at[step],
            recv_sem=pay_recv.at[step],
            device_id=(flipped(me, SUM_BITS[step]),),
            device_id_type=MESH,
        )

    def block(src, dst, pair, k):
        rows = pl.ds(k * CHUNK, CHUNK)
        feat = src[...]
        gain = gt_ref[...]
        scaled = feat * gain
        norm = jnp.sqrt(jnp.sum(scaled * scaled, axis=-1, keepdims=True) + eps)
        emb = scaled / norm
        e_all[pair, rows] = emb
        image = img_emb[...]
        dots = matmul(emb, image, (1, 1))
        logits = mult * dots + offs
        small = jnp.exp(-jnp.abs(logits))
        loss = jnp.maximum(logits, 0.0) + jnp.log1p(small)
        g = jnp.where(logits >= 0.0, 1.0, small) / (1.0 + small)
        if pair == SELF:
            text_row = k * CHUNK + lax.broadcasted_iota(jnp.int32, (CHUNK, ROWS), 0)
            image_row = lax.broadcasted_iota(jnp.int32, (CHUNK, ROWS), 1)
            labels = (text_row == image_row).astype(jnp.float32)
            loss = loss - labels * logits
            g = g - labels
        g_all[pair, rows] = g
        for i, term in enumerate((loss, g * dots, g)):
            line = jnp.sum(term, axis=0, keepdims=True)
            sum_acc[i : i + 1] += line[:, :LANES] + line[:, LANES:]
        d_emb = mult * matmul(g, image, (1, 0))
        d_scaled = (d_emb - emb * jnp.sum(emb * d_emb, axis=-1, keepdims=True)) / norm
        dst[...] = d_scaled * gain
        gain_acc[...] += jnp.sum(d_scaled * feat, axis=0, keepdims=True)

    def image_side(pair):
        for half in range(2):
            cols = pl.ds(half * CHUNK, CHUNK)
            part = mult * matmul(g_all[pair, :, cols], e_all[pair], (0, 0))
            if pair == SELF:
                d_img[cols] = part
            else:
                d_img[cols] += part

    def image_norm():
        for half in range(2):
            rows = pl.ds(half * CHUNK, CHUNK)
            scaled = img_raw[rows] * gi_ref[...]
            norm = jnp.sqrt(jnp.sum(scaled * scaled, axis=-1, keepdims=True) + eps)
            img_emb[rows] = scaled / norm

    def image_finish():
        total = jnp.zeros((1, D), jnp.float32)
        for half in range(2):
            rows = pl.ds(half * CHUNK, CHUNK)
            feat = img_raw[rows]
            gain = gi_ref[...]
            scaled = feat * gain
            norm = jnp.sqrt(jnp.sum(scaled * scaled, axis=-1, keepdims=True) + eps)
            emb = img_emb[rows]
            d_emb = d_img[rows]
            d_scaled = (
                d_emb - emb * jnp.sum(emb * d_emb, axis=-1, keepdims=True)
            ) / norm
            img_grad_ref[rows] = d_scaled * gain
            total = total + jnp.sum(d_scaled * feat, axis=0, keepdims=True)
        text = gain_acc[...]
        pay[0] = jnp.zeros((PAY, LANES), jnp.float32)
        for i in range(TILES):
            pay[0, i : i + 1] = total[:, i * LANES : (i + 1) * LANES]
            pay[0, TILES + i : TILES + i + 1] = text[:, i * LANES : (i + 1) * LANES]
        pay[0, 2 * TILES : 2 * TILES + 3] = sum_acc[0:3]

    def sum_step(step):
        pay_copy(step).wait_recv()
        pay[step + 1] = pay[step] + pay_in[step]

    def sum_finish():
        total = pay[BITS]
        for i in range(TILES):
            cols = pl.ds(i * LANES, LANES)
            img_gain_ref[:, cols] = total[i : i + 1]
            txt_gain_ref[:, cols] = total[TILES + i : TILES + i + 1]
        for i in range(3):
            line = total[2 * TILES + i : 2 * TILES + i + 1]
            sums_ref[i] = jnp.sum(line) / (3.0 * ROWS * ROWS * (1 << BITS))

    def self_block(k):
        rows = pl.ds(k * CHUNK, CHUNK)
        block(txt_raw.at[rows], txt_grad_ref.at[rows], SELF, k)

    def far_block(k):
        rows = pl.ds(k * CHUNK, CHUNK)
        far_copy(0, k, txt_hbm, far_in).wait_recv()
        block(far_in.at[rows], far_ret.at[rows], FAR, k)
        far_copy(1, k, far_ret, far_back).start()

    def far_add(k):
        rows = pl.ds(k * CHUNK, CHUNK)
        far_copy(1, k, far_ret, far_back).wait_recv()
        txt_grad_ref[rows] += far_back[rows]

    for k in range(CHUNKS):
        for d in range(2):
            hop(0, 0, k, d, txt_hbm.at[pl.ds(k * CHUNK + d * HALF, HALF)]).start()
    for k in range(CHUNKS):
        far_copy(0, k, txt_hbm, far_in).start()
    loads = [
        pltpu.make_async_copy(img_hbm, img_raw, load_sem.at[0]),
        pltpu.make_async_copy(txt_hbm, txt_raw, load_sem.at[1]),
    ]
    for load in loads:
        load.start()
    gain_acc[...] = jnp.zeros_like(gain_acc)
    sum_acc[...] = jnp.zeros_like(sum_acc)
    for load in loads:
        load.wait()
    image_norm()

    work = {
        0: lambda: self_block(0),
        1: lambda: self_block(1),
        2: lambda: image_side(SELF),
        5: lambda: far_block(0),
        6: lambda: far_block(1),
        7: lambda: image_side(FAR),
        12: lambda: far_add(0),
        13: lambda: far_add(1),
    }
    for h in range(HOPS - 1):
        for k in range(CHUNKS):
            forward(0, h, k)
            work.get(h * CHUNKS + k, lambda: None)()

    for k in range(CHUNKS):
        for d in range(2):
            hop(0, HOPS - 1, k, d, landed(0, HOPS - 1, k, d)).wait_recv()
        block(hops.at[0, HOPS - 1, k], ret.at[k], NEAR, k)
        for d in range(2):
            hop(1, 0, k, d, ret.at[k, pl.ds(d * HALF, HALF)]).start()

    image_side(NEAR)
    image_finish()
    pay_copy(0).start()
    for h in range(HOPS - 1):
        for k in range(CHUNKS):
            forward(1, h, k)
            step = h * CHUNKS + k - 1
            if 0 <= step < BITS:
                sum_step(step)
                if step + 1 < BITS:
                    pay_copy(step + 1).start()
            if step == BITS:
                sum_finish()
            sent(0, h, k)

    for k in range(CHUNKS):
        for d in range(2):
            hop(1, HOPS - 1, k, d, landed(1, HOPS - 1, k, d)).wait_recv()
        rows = pl.ds(k * CHUNK, CHUNK)
        txt_grad_ref[rows] += hops[1, HOPS - 1, k]

    for k in range(CHUNKS):
        sent(0, HOPS - 1, k)
        for h in range(HOPS):
            sent(1, h, k)
        far_copy(0, k, txt_hbm, far_in).wait_send()
        far_copy(1, k, far_ret, far_back).wait_send()
    for step in range(BITS):
        pay_copy(step).wait_send()


def shards(
    picture_encoder_result,
    caption_encoder_result,
    picture_channel_factor,
    caption_channel_factor,
    logit_multiplier,
    logit_offset,
):
    f32 = jnp.float32
    vmem = pl.BlockSpec(memory_space=pltpu.VMEM)
    smem = pl.BlockSpec(memory_space=pltpu.SMEM)
    hbm = pl.BlockSpec(memory_space=pl.ANY)
    dma = pltpu.SemaphoreType.DMA
    image_grad, text_grad, image_gain, text_gain, sums = pl.pallas_call(
        kernel,
        name="contrast",
        out_shape=(
            jax.ShapeDtypeStruct((ROWS, D), f32),
            jax.ShapeDtypeStruct((ROWS, D), f32),
            jax.ShapeDtypeStruct((1, D), f32),
            jax.ShapeDtypeStruct((1, D), f32),
            jax.ShapeDtypeStruct((3,), f32),
        ),
        in_specs=[smem, smem, hbm, hbm, vmem, vmem],
        out_specs=(vmem, vmem, vmem, vmem, smem),
        scratch_shapes=[
            pltpu.VMEM((ROWS, D), f32),
            pltpu.VMEM((ROWS, D), f32),
            pltpu.VMEM((ROWS, D), f32),
            pltpu.VMEM((ROWS, D), f32),
            pltpu.VMEM((2, HOPS, CHUNKS, CHUNK, D), f32),
            pltpu.VMEM((CHUNKS, CHUNK, D), f32),
            pltpu.VMEM((ROWS, D), f32),
            pltpu.VMEM((ROWS, D), f32),
            pltpu.VMEM((ROWS, D), f32),
            pltpu.VMEM((3, ROWS, ROWS), f32),
            pltpu.VMEM((3, ROWS, D), f32),
            pltpu.VMEM((1, D), f32),
            pltpu.VMEM((8, LANES), f32),
            pltpu.VMEM((BITS + 1, PAY, LANES), f32),
            pltpu.VMEM((BITS, PAY, LANES), f32),
            dma((2,)),
            dma((2, HOPS, CHUNKS, 2)),
            dma((2, HOPS, CHUNKS, 2)),
            dma((2, CHUNKS)),
            dma((2, CHUNKS)),
            dma((BITS,)),
            dma((BITS,)),
        ],
        compiler_params=pltpu.CompilerParams(
            collective_id=0, has_side_effects=True, vmem_limit_bytes=52 << 20
        ),
        cost_estimate=pl.CostEstimate(
            flops=18 * ROWS * ROWS * D,
            bytes_accessed=16 * ROWS * D,
            transcendentals=6 * ROWS * ROWS,
        ),
    )(
        logit_multiplier.reshape(1),
        logit_offset.reshape(1),
        picture_encoder_result,
        caption_encoder_result,
        picture_channel_factor.reshape(1, D),
        caption_channel_factor.reshape(1, D),
    )
    return (
        image_grad,
        text_grad,
        image_gain.reshape(D),
        text_gain.reshape(D),
        sums[1],
        sums[2],
        sums[0],
    )


def solution(mesh):
    return jax.shard_map(
        shards,
        mesh=mesh,
        in_specs=(P("dp", None), P("dp", None), P(), P(), P(), P()),
        out_specs=(P("dp", None), P("dp", None), P(), P(), P(), P(), P()),
        check_vma=False,
    )
```

```python
import functools

import jax
import jax.numpy as jnp
from jax import lax
from jax.experimental import pallas as pl
from jax.experimental.pallas import tpu as pltpu
from jax.sharding import PartitionSpec as P

eps = 1e-06
MESH = pl.DeviceIdType.MESH

ROWS = 256
D = 1152
CHUNKS = 2
CHUNK = ROWS // CHUNKS
HALF = CHUNK // 2
Z = 16
HOPS = Z // 2
BITS = 9
FAR_BIT = 8
NEAR_BIT = 4
CROSS_BITS = (2, 3, 4, 5, 6, 7, 8)
SUM_BITS = (1, 2, 3, 4, 5, 6, 7, 8)
SUM_SLOTS = (0, 1, 2, 3, 4, 5, 7, 9, 11, 12)
FAR_SLOTS = (10, 13)
LANES = 128
TILES = D // LANES
PAY = TILES + 2
SELF, FAR, NEAR = 0, 1, 2


def flipped(me, bit):
    stride = 1 << bit
    return me + stride - 2 * stride * ((me // stride) % 2)


def z_shifted(me, step):
    z = (me // 2) % Z
    return me + 2 * ((z + step + Z) % Z - z)


def matmul(a, b, contract):
    return lax.dot_general(
        a,
        b,
        ((contract[:1], contract[1:]), ((), ())),
        precision=lax.Precision.HIGHEST,
        preferred_element_type=jnp.float32,
    )


def kernel(
    mult_hbm,
    offs_hbm,
    img_hbm,
    txt_hbm,
    gi_hbm,
    gt_hbm,
    img_grad_ref,
    txt_grad_ref,
    total_ref,
    mult_ref,
    offs_ref,
    gi_ref,
    gt_ref,
    img_raw,
    txt_raw,
    img_emb,
    d_img,
    hops,
    ret,
    far_in,
    far_ret,
    far_back,
    g_all,
    e_all,
    gain_acc,
    sum_acc,
    pay_all,
    pay,
    pay_in,
    ready,
    load_sem,
    send_sem,
    recv_sem,
    far_send,
    far_recv,
    pay_send,
    pay_recv,
):
    me = lax.axis_index("dp")
    core = me % 2
    mate = flipped(me, 0)
    ways = (z_shifted(me, 1), z_shifted(me, -1))
    far = flipped(me, FAR_BIT)

    def greet(sem, other):
        pl.semaphore_signal(sem, inc=1, device_id=(other,), device_id_type=MESH)

    barrier = pltpu.get_barrier_semaphore()
    for other in ways:
        greet(barrier, other - core)
    for bit in CROSS_BITS:
        greet(barrier, flipped(me, bit) - core + 1)

    @pl.when(core == 1)
    def _():
        greet(barrier, mate)
        pl.semaphore_wait(ready, 1)

    @pl.when(core == 0)
    def _():
        pl.semaphore_wait(barrier, 5)
        greet(ready, mate)

    def meet_others():
        @pl.when(core == 1)
        def _():
            pl.semaphore_wait(barrier, 2 * len(CROSS_BITS))
            greet(ready, mate)

        @pl.when(core == 0)
        def _():
            pl.semaphore_wait(ready, 1)

    def hop(phase, h, k, d, src):
        return pltpu.make_async_remote_copy(
            src_ref=src,
            dst_ref=hops.at[phase, h, k, pl.ds(d * HALF, HALF)],
            send_sem=send_sem.at[phase, h, k, d],
            recv_sem=recv_sem.at[phase, h, k, d],
            device_id=(ways[d],),
            device_id_type=MESH,
        )

    def landed(phase, h, k, d):
        return hops.at[phase, h, k, pl.ds(d * HALF, HALF)]

    def forward(phase, h, k):
        for d in range(2):
            src = landed(phase, h, k, d)
            hop(phase, h, k, d, src).wait_recv()
            hop(phase, h + 1, k, d, src).start()

    def sent(phase, h, k):
        for d in range(2):
            hop(phase, h, k, d, landed(phase, h, k, d)).wait_send()

    def far_copy(leg, k, src, dst):
        return pltpu.make_async_remote_copy(
            src_ref=src.at[pl.ds(k * CHUNK, CHUNK)],
            dst_ref=dst.at[pl.ds(k * CHUNK, CHUNK)],
            send_sem=far_send.at[leg, k],
            recv_sem=far_recv.at[leg, k],
            device_id=(far,),
            device_id_type=MESH,
        )

    def pay_copy(step):
        first, last = step == 0, step == len(SUM_BITS) + 1
        return pltpu.make_async_remote_copy(
            src_ref=pay_all.at[1 - core] if first else pay.at[step - 1],
            dst_ref=total_ref.at[core] if last else pay_in.at[step],
            send_sem=pay_send.at[step],
            recv_sem=pay_recv.at[step],
            device_id=(mate if first or last else flipped(me, SUM_BITS[step - 1]),),
            device_id_type=MESH,
        )

    def block(src, dst, pair, k):
        rows = pl.ds(k * CHUNK, CHUNK)
        feat = src[...]
        gain = gt_ref[...].reshape(1, D)
        scaled = feat * gain
        norm = jnp.sqrt(jnp.sum(scaled * scaled, axis=-1, keepdims=True) + eps)
        emb = scaled / norm
        e_all[pair, rows] = emb
        image = img_emb[...]
        dots = matmul(emb, image, (1, 1))
        logits = mult * dots + offs
        small = jnp.exp(-jnp.abs(logits))
        loss = jnp.maximum(logits, 0.0) + jnp.log1p(small)
        g = jnp.where(logits >= 0.0, 1.0, small) / (1.0 + small)
        if pair == SELF:
            text_row = k * CHUNK + lax.broadcasted_iota(jnp.int32, (CHUNK, ROWS), 0)
            image_row = lax.broadcasted_iota(jnp.int32, (CHUNK, ROWS), 1)
            labels = (text_row == image_row).astype(jnp.float32)
            loss = loss - labels * logits
            g = g - labels
        g_all[pair, rows] = g
        for i, term in enumerate((loss, g * dots, g)):
            line = jnp.sum(term, axis=0, keepdims=True)
            sum_acc[i : i + 1] += line[:, :LANES] + line[:, LANES:]
        d_emb = mult * matmul(g, image, (1, 0))
        d_scaled = (d_emb - emb * jnp.sum(emb * d_emb, axis=-1, keepdims=True)) / norm
        dst[...] = d_scaled * gain
        gain_acc[...] += jnp.sum(d_scaled * feat, axis=0, keepdims=True)

    def image_side(pair):
        for half in range(2):
            cols = pl.ds(half * CHUNK, CHUNK)
            part = mult * matmul(g_all[pair, :, cols], e_all[pair], (0, 0))
            if pair == SELF:
                d_img[cols] = part
            else:
                d_img[cols] += part

    def image_norm():
        for half in range(2):
            rows = pl.ds(half * CHUNK, CHUNK)
            scaled = img_raw[rows] * gi_ref[...].reshape(1, D)
            norm = jnp.sqrt(jnp.sum(scaled * scaled, axis=-1, keepdims=True) + eps)
            img_emb[rows] = scaled / norm

    def image_finish():
        total = jnp.zeros((1, D), jnp.float32)
        for half in range(2):
            rows = pl.ds(half * CHUNK, CHUNK)
            feat = img_raw[rows]
            gain = gi_ref[...].reshape(1, D)
            scaled = feat * gain
            norm = jnp.sqrt(jnp.sum(scaled * scaled, axis=-1, keepdims=True) + eps)
            emb = img_emb[rows]
            d_emb = d_img[rows]
            d_scaled = (
                d_emb - emb * jnp.sum(emb * d_emb, axis=-1, keepdims=True)
            ) / norm
            img_grad_ref[rows] = d_scaled * gain
            total = total + jnp.sum(d_scaled * feat, axis=0, keepdims=True)
        text = gain_acc[...]
        for i in range(TILES):
            pay_all[0, i] = total[:, i * LANES : (i + 1) * LANES]
            pay_all[1, i] = text[:, i * LANES : (i + 1) * LANES]
        pay_all[0, TILES] = sum_acc[0:1]
        pay_all[0, TILES + 1] = sum_acc[1:2]
        pay_all[1, TILES] = sum_acc[2:3]
        pay_all[1, TILES + 1] = jnp.zeros((1, LANES), jnp.float32)

    def sum_step(step):
        last = len(SUM_BITS) + 1
        pay_copy(step).wait_recv()
        if step == 0:
            pay[0] = pay_all[core] + pay_in[0]
        elif step < last:
            pay[step] = pay[step - 1] + pay_in[step]
        if step == last - 1:
            total_ref[core] = pay[step]
        if step < last:
            pay_copy(step + 1).start()

    def self_block(k):
        rows = pl.ds(k * CHUNK, CHUNK)
        block(txt_raw.at[rows], txt_grad_ref.at[rows], SELF, k)

    def far_block(k):
        rows = pl.ds(k * CHUNK, CHUNK)
        far_copy(0, k, txt_hbm, far_in).wait_recv()
        block(far_in.at[rows], far_ret.at[rows], FAR, k)
        far_copy(1, k, far_ret, far_back).start()

    def far_add(k):
        rows = pl.ds(k * CHUNK, CHUNK)
        far_copy(1, k, far_ret, far_back).wait_recv()
        txt_grad_ref[rows] += far_back[rows]

    for k in range(CHUNKS):
        for d in range(2):
            hop(0, 0, k, d, txt_hbm.at[pl.ds(k * CHUNK + d * HALF, HALF)]).start()
    loads = [
        pltpu.make_async_copy(src, dst, load_sem.at[i])
        for i, (src, dst) in enumerate(
            (
                (mult_hbm, mult_ref),
                (offs_hbm, offs_ref),
                (gi_hbm, gi_ref),
                (gt_hbm, gt_ref),
                (img_hbm, img_raw),
                (txt_hbm, txt_raw),
            )
        )
    ]
    for load in loads:
        load.start()
    gain_acc[...] = jnp.zeros_like(gain_acc)
    sum_acc[...] = jnp.zeros_like(sum_acc)
    for load in loads:
        load.wait()
    mult = mult_ref[0]
    offs = offs_ref[0]
    image_norm()

    def far_start():
        meet_others()
        for k in range(CHUNKS):
            far_copy(0, k, txt_hbm, far_in).start()

    work = {
        0: lambda: self_block(0),
        1: lambda: self_block(1),
        2: far_start,
        3: lambda: image_side(SELF),
        9: lambda: far_block(0),
        10: lambda: far_block(1),
        11: lambda: image_side(FAR),
    }
    for h in range(HOPS - 1):
        for k in range(CHUNKS):
            forward(0, h, k)
            work.get(h * CHUNKS + k, lambda: None)()

    for k in range(CHUNKS):
        for d in range(2):
            hop(0, HOPS - 1, k, d, landed(0, HOPS - 1, k, d)).wait_recv()
        block(hops.at[0, HOPS - 1, k], ret.at[k], NEAR, k)
        for d in range(2):
            hop(1, 0, k, d, ret.at[k, pl.ds(d * HALF, HALF)]).start()

    image_side(NEAR)
    image_finish()
    pay_copy(0).start()
    for h in range(HOPS - 1):
        for k in range(CHUNKS):
            forward(1, h, k)
            slot = h * CHUNKS + k
            if slot in SUM_SLOTS:
                sum_step(SUM_SLOTS.index(slot))
            if slot in FAR_SLOTS:
                far_add(FAR_SLOTS.index(slot))
            sent(0, h, k)

    for k in range(CHUNKS):
        for d in range(2):
            hop(1, HOPS - 1, k, d, landed(1, HOPS - 1, k, d)).wait_recv()
        rows = pl.ds(k * CHUNK, CHUNK)
        txt_grad_ref[rows] += hops[1, HOPS - 1, k]

    for k in range(CHUNKS):
        sent(0, HOPS - 1, k)
        for h in range(HOPS):
            sent(1, h, k)
        far_copy(0, k, txt_hbm, far_in).wait_send()
        far_copy(1, k, far_ret, far_back).wait_send()
    for step in range(len(SUM_SLOTS)):
        pay_copy(step).wait_send()


def finish(
    img_ref, txt_ref, total_ref, img_out, txt_out, gi_out, gt_out, *rest
):
    sums_out, sems = rest[:3], rest[3]
    copies = [
        pltpu.make_async_copy(img_ref, img_out, sems.at[0]),
        pltpu.make_async_copy(txt_ref, txt_out, sems.at[1]),
    ]
    for copy in copies:
        copy.start()
    for i in range(TILES):
        cols = pl.ds(i * LANES, LANES)
        gi_out[cols] = total_ref[0, i, 0]
        gt_out[cols] = total_ref[1, i, 0]
    for out, line in zip(
        sums_out, (total_ref[0, TILES + 1], total_ref[1, TILES], total_ref[0, TILES])
    ):
        out[...] = jnp.sum(line, axis=-1, keepdims=True) / (
            3.0 * ROWS * ROWS * (1 << BITS)
        )
    for copy in copies:
        copy.wait()


def shards(
    picture_encoder_result,
    caption_encoder_result,
    picture_channel_factor,
    caption_channel_factor,
    logit_multiplier,
    logit_offset,
):
    f32 = jnp.float32
    vmem = pl.BlockSpec(memory_space=pltpu.VMEM)
    hbm = pl.BlockSpec(memory_space=pltpu.HBM)
    dma = pltpu.SemaphoreType.DMA
    wide = jax.ShapeDtypeStruct((ROWS, D), f32)
    image_grad, text_grad, total = pl.pallas_call(
        kernel,
        name="contrast",
        out_shape=(
            wide,
            wide,
            jax.ShapeDtypeStruct((2, PAY, 1, LANES), f32),
        ),
        in_specs=[hbm] * 6,
        out_specs=(vmem, vmem, vmem),
        scratch_shapes=[
            pltpu.SMEM((1,), f32),
            pltpu.SMEM((1,), f32),
            pltpu.VMEM((D,), f32),
            pltpu.VMEM((D,), f32),
            pltpu.VMEM((ROWS, D), f32),
            pltpu.VMEM((ROWS, D), f32),
            pltpu.VMEM((ROWS, D), f32),
            pltpu.VMEM((ROWS, D), f32),
            pltpu.VMEM((2, HOPS, CHUNKS, CHUNK, D), f32),
            pltpu.VMEM((CHUNKS, CHUNK, D), f32),
            pltpu.VMEM((ROWS, D), f32),
            pltpu.VMEM((ROWS, D), f32),
            pltpu.VMEM((ROWS, D), f32),
            pltpu.VMEM((3, ROWS, ROWS), f32),
            pltpu.VMEM((3, ROWS, D), f32),
            pltpu.VMEM((1, D), f32),
            pltpu.VMEM((8, LANES), f32),
            pltpu.VMEM((2, PAY, 1, LANES), f32),
            pltpu.VMEM((len(SUM_SLOTS) - 1, PAY, 1, LANES), f32),
            pltpu.VMEM((len(SUM_SLOTS) - 1, PAY, 1, LANES), f32),
            pltpu.SemaphoreType.REGULAR,
            dma((6,)),
            dma((2, HOPS, CHUNKS, 2)),
            dma((2, HOPS, CHUNKS, 2)),
            dma((2, CHUNKS)),
            dma((2, CHUNKS)),
            dma((len(SUM_SLOTS),)),
            dma((len(SUM_SLOTS),)),
        ],
        compiler_params=pltpu.CompilerParams(
            collective_id=0, has_side_effects=True, vmem_limit_bytes=51 << 20
        ),
        cost_estimate=pl.CostEstimate(
            flops=18 * ROWS * ROWS * D,
            bytes_accessed=16 * ROWS * D,
            transcendentals=6 * ROWS * ROWS,
        ),
    )(
        logit_multiplier.reshape(1),
        logit_offset.reshape(1),
        picture_encoder_result,
        caption_encoder_result,
        pltpu.with_memory_space_constraint(picture_channel_factor, pltpu.HBM),
        pltpu.with_memory_space_constraint(caption_channel_factor, pltpu.HBM),
    )
    one = jax.ShapeDtypeStruct((1, 1), f32)
    line = jax.ShapeDtypeStruct((D,), f32)
    *results, temp, bias, loss = pl.pallas_call(
        finish,
        name="results",
        out_shape=(wide, wide, line, line, one, one, one),
        in_specs=[vmem] * 3,
        out_specs=(hbm, hbm, vmem, vmem, vmem, vmem, vmem),
        scratch_shapes=[dma((2,))],
        compiler_params=pltpu.CompilerParams(vmem_limit_bytes=8 << 20),
    )(image_grad, text_grad, total)
    return (*results, temp[0, 0], bias[0, 0], loss[0, 0])


def solution(mesh):
    return jax.shard_map(
        shards,
        mesh=mesh,
        in_specs=(P("dp", None), P("dp", None), P(), P(), P(), P()),
        out_specs=(P("dp", None), P("dp", None), P(), P(), P(), P(), P()),
        check_vma=False,
    )
```

```python
import functools

import jax
import jax.numpy as jnp
from jax import lax
from jax.experimental import pallas as pl
from jax.experimental.pallas import tpu as pltpu
from jax.sharding import PartitionSpec as P

eps = 1e-06
MESH = pl.DeviceIdType.MESH

ROWS = 256
D = 1152
CHUNKS = 2
CHUNK = ROWS // CHUNKS
HALF = CHUNK // 2
Z = 16
HOPS = Z // 2
BITS = 9
FAR_BIT = 8
NEAR_BIT = 4
CROSS_BITS = (5, 6, 7, 8)
SUM_BITS = (0, 1, 2, 3, 4, 5, 6, 7, 8, 4, 0)
ACROSS = len(SUM_BITS) - 2
SUM_SLOTS = (2, 3, 4, 5, 7, 8, 9, 10, 11, 13, 14)
FAR_SLOTS = (8, 12)
LANES = 128
TILES = D // LANES
PAY = TILES + 2
SELF, FAR, NEAR = 0, 1, 2


def flipped(me, bit):
    stride = 1 << bit
    return me + stride - 2 * stride * ((me // stride) % 2)


def z_shifted(me, step):
    z = (me // 2) % Z
    return me + 2 * ((z + step + Z) % Z - z)


def matmul(a, b, contract):
    return lax.dot_general(
        a,
        b,
        ((contract[:1], contract[1:]), ((), ())),
        precision=lax.Precision.HIGHEST,
        preferred_element_type=jnp.float32,
    )


def kernel(
    mult_hbm,
    offs_hbm,
    img_hbm,
    txt_hbm,
    gi_hbm,
    gt_hbm,
    img_grad_ref,
    txt_grad_ref,
    total_ref,
    mult_ref,
    offs_ref,
    gi_ref,
    gt_ref,
    img_raw,
    txt_raw,
    img_emb,
    d_img,
    hops,
    ret,
    far_in,
    far_ret,
    far_back,
    g_all,
    e_all,
    gain_acc,
    sum_acc,
    pay_all,
    pay,
    pay_in,
    ready,
    quarter,
    far_in_kernel,
    load_sem,
    send_sem,
    recv_sem,
    far_send,
    far_recv,
    pay_send,
    pay_recv,
):
    me = lax.axis_index("dp")
    core = me % 2
    mate = flipped(me, 0)
    ways = (z_shifted(me, 1), z_shifted(me, -1))
    far = flipped(me, FAR_BIT)

    def greet(sem, other):
        pl.semaphore_signal(sem, inc=1, device_id=(other,), device_id_type=MESH)

    place = (me // 2) % Z
    lower = place < HOPS
    upper = place >= HOPS
    barrier = pltpu.get_barrier_semaphore()
    for other in ways:
        greet(barrier, other - core * (1 - (other // 2) % Z // HOPS))

    @pl.when(upper)
    def _():
        greet(barrier, mate)
        pl.semaphore_wait(barrier, 3)

    @pl.when(lower)
    def _():
        for bit in CROSS_BITS:
            greet(barrier, flipped(me, bit) - core + 1)

    @pl.when(lower & (core == 1))
    def _():
        greet(barrier, mate)
        pl.semaphore_wait(ready, 1)

    @pl.when(lower & (core == 0))
    def _():
        pl.semaphore_wait(barrier, 5)
        greet(ready, mate)

    def meet_others():
        @pl.when(core == 1)
        def _():
            pl.semaphore_wait(barrier, 2 * len(CROSS_BITS))
            greet(ready, mate)

        @pl.when(core == 0)
        def _():
            pl.semaphore_wait(ready, 1)

    def at_ends(act):
        @pl.when(place == 0)
        def _():
            act(-1)

        @pl.when(place == HOPS - 1)
        def _():
            act(1)

    def quarter_in(_):
        greet(quarter, far)

    def tell_quarter(way):
        pl.semaphore_wait(quarter, 1)
        for i in range(1, HOPS // 2 + 1):
            greet(far_in_kernel, z_shifted(me, way * i))

    def hop(phase, h, k, d, src):
        return pltpu.make_async_remote_copy(
            src_ref=src,
            dst_ref=hops.at[phase, h, k, pl.ds(d * HALF, HALF)],
            send_sem=send_sem.at[phase, h, k, d],
            recv_sem=recv_sem.at[phase, h, k, d],
            device_id=(ways[d],),
            device_id_type=MESH,
        )

    def landed(phase, h, k, d):
        return hops.at[phase, h, k, pl.ds(d * HALF, HALF)]

    def forward(phase, h, k):
        for d in range(2):
            src = landed(phase, h, k, d)
            hop(phase, h, k, d, src).wait_recv()
            hop(phase, h + 1, k, d, src).start()

    def sent(phase, h, k):
        for d in range(2):
            hop(phase, h, k, d, landed(phase, h, k, d)).wait_send()

    def far_copy(leg, k, src, dst):
        return pltpu.make_async_remote_copy(
            src_ref=src.at[pl.ds(k * CHUNK, CHUNK)],
            dst_ref=dst.at[pl.ds(k * CHUNK, CHUNK)],
            send_sem=far_send.at[leg, k],
            recv_sem=far_recv.at[leg, k],
            device_id=(far,),
            device_id_type=MESH,
        )

    def pay_copy(step):
        first, last = step == 0, step == len(SUM_BITS) - 1
        return pltpu.make_async_remote_copy(
            src_ref=pay_all.at[1 - core] if first else pay.at[step - 1],
            dst_ref=total_ref.at[core] if last else pay_in.at[step],
            send_sem=pay_send.at[step],
            recv_sem=pay_recv.at[step],
            device_id=(flipped(me, SUM_BITS[step]),),
            device_id_type=MESH,
        )

    def on_senders(step, act):
        if step <= 4 or step > ACROSS:
            act()
        else:
            pl.when(lower)(act)

    def on_receivers(step, act):
        if step == ACROSS:
            pl.when(upper)(act)
        else:
            on_senders(step, act)

    def block(src, dst, pair, k):
        rows = pl.ds(k * CHUNK, CHUNK)
        feat = src[...]
        gain = gt_ref[...].reshape(1, D)
        scaled = feat * gain
        norm = jnp.sqrt(jnp.sum(scaled * scaled, axis=-1, keepdims=True) + eps)
        emb = scaled / norm
        e_all[pair, rows] = emb
        image = img_emb[...]
        dots = matmul(emb, image, (1, 1))
        logits = mult * dots + offs
        small = jnp.exp(-jnp.abs(logits))
        loss = jnp.maximum(logits, 0.0) + jnp.log1p(small)
        g = jnp.where(logits >= 0.0, 1.0, small) / (1.0 + small)
        if pair == SELF:
            text_row = k * CHUNK + lax.broadcasted_iota(jnp.int32, (CHUNK, ROWS), 0)
            image_row = lax.broadcasted_iota(jnp.int32, (CHUNK, ROWS), 1)
            labels = (text_row == image_row).astype(jnp.float32)
            loss = loss - labels * logits
            g = g - labels
        g_all[pair, rows] = g
        for i, term in enumerate((loss, g * dots, g)):
            line = jnp.sum(term, axis=0, keepdims=True)
            sum_acc[i : i + 1] += line[:, :LANES] + line[:, LANES:]
        d_emb = mult * matmul(g, image, (1, 0))
        d_scaled = (d_emb - emb * jnp.sum(emb * d_emb, axis=-1, keepdims=True)) / norm
        dst[...] = d_scaled * gain
        gain_acc[...] += jnp.sum(d_scaled * feat, axis=0, keepdims=True)

    def image_side(pair):
        for half in range(2):
            cols = pl.ds(half * CHUNK, CHUNK)
            part = mult * matmul(g_all[pair, :, cols], e_all[pair], (0, 0))
            if pair == SELF:
                d_img[cols] = part
            else:
                d_img[cols] += part

    def image_norm():
        for half in range(2):
            rows = pl.ds(half * CHUNK, CHUNK)
            scaled = img_raw[rows] * gi_ref[...].reshape(1, D)
            norm = jnp.sqrt(jnp.sum(scaled * scaled, axis=-1, keepdims=True) + eps)
            img_emb[rows] = scaled / norm

    def image_finish():
        total = jnp.zeros((1, D), jnp.float32)
        for half in range(2):
            rows = pl.ds(half * CHUNK, CHUNK)
            feat = img_raw[rows]
            gain = gi_ref[...].reshape(1, D)
            scaled = feat * gain
            norm = jnp.sqrt(jnp.sum(scaled * scaled, axis=-1, keepdims=True) + eps)
            emb = img_emb[rows]
            d_emb = d_img[rows]
            d_scaled = (
                d_emb - emb * jnp.sum(emb * d_emb, axis=-1, keepdims=True)
            ) / norm
            img_grad_ref[rows] = d_scaled * gain
            total = total + jnp.sum(d_scaled * feat, axis=0, keepdims=True)
        text = gain_acc[...]
        for i in range(TILES):
            pay_all[0, i] = total[:, i * LANES : (i + 1) * LANES]
            pay_all[1, i] = text[:, i * LANES : (i + 1) * LANES]
        pay_all[0, TILES] = sum_acc[0:1]
        pay_all[0, TILES + 1] = sum_acc[1:2]
        pay_all[1, TILES] = sum_acc[2:3]
        pay_all[1, TILES + 1] = jnp.zeros((1, LANES), jnp.float32)

    def sum_step(step):
        last = len(SUM_BITS) - 1

        def take():
            pay_copy(step).wait_recv()
            if step == 0:
                pay[0] = pay_all[core] + pay_in[0]
            elif step < ACROSS:
                pay[step] = pay[step - 1] + pay_in[step]
            elif step == ACROSS:
                pay[step] = pay_in[step]

        on_receivers(step, take)
        if step == ACROSS:

            @pl.when(lower)
            def _():
                pay[step] = pay[step - 1]

            total_ref[core] = pay[step]
        if step < last:
            on_senders(step + 1, lambda: pay_copy(step + 1).start())

    def self_block(k):
        rows = pl.ds(k * CHUNK, CHUNK)
        block(txt_raw.at[rows], txt_grad_ref.at[rows], SELF, k)

    def far_block(k):
        rows = pl.ds(k * CHUNK, CHUNK)
        far_copy(0, k, txt_hbm, far_in).wait_recv()
        block(far_in.at[rows], far_ret.at[rows], FAR, k)
        far_copy(1, k, far_ret, far_back).start()

    def far_add(k):
        rows = pl.ds(k * CHUNK, CHUNK)
        far_copy(1, k, far_ret, far_back).wait_recv()
        txt_grad_ref[rows] += far_back[rows]

    for k in range(CHUNKS):
        for d in range(2):
            hop(0, 0, k, d, txt_hbm.at[pl.ds(k * CHUNK + d * HALF, HALF)]).start()
    loads = [
        pltpu.make_async_copy(src, dst, load_sem.at[i])
        for i, (src, dst) in enumerate(
            (
                (mult_hbm, mult_ref),
                (offs_hbm, offs_ref),
                (gi_hbm, gi_ref),
                (gt_hbm, gt_ref),
                (img_hbm, img_raw),
                (txt_hbm, txt_raw),
            )
        )
    ]
    for load in loads:
        load.start()
    gain_acc[...] = jnp.zeros_like(gain_acc)
    sum_acc[...] = jnp.zeros_like(sum_acc)
    for load in loads:
        load.wait()
    mult = mult_ref[0]
    offs = offs_ref[0]
    image_norm()

    def far_start():
        for k in range(CHUNKS):
            far_copy(0, k, txt_hbm, far_in).start()

    def lower_start():
        @pl.when(lower)
        def _():
            meet_others()
            far_start()

    def upper_start():
        @pl.when(upper)
        def _():
            pl.semaphore_wait(far_in_kernel, 1)
            far_start()

    work = {
        0: lambda: self_block(0),
        1: lambda: self_block(1),
        2: lower_start,
        3: lambda: image_side(SELF),
        HOPS - 1: lambda: at_ends(quarter_in),
        HOPS: lambda: at_ends(tell_quarter),
        HOPS + 2: upper_start,
    }
    for h in range(HOPS - 1):
        for k in range(CHUNKS):
            forward(0, h, k)
            work.get(h * CHUNKS + k, lambda: None)()

    for k in range(CHUNKS):
        for d in range(2):
            hop(0, HOPS - 1, k, d, landed(0, HOPS - 1, k, d)).wait_recv()
        block(hops.at[0, HOPS - 1, k], ret.at[k], NEAR, k)
        for d in range(2):
            hop(1, 0, k, d, ret.at[k, pl.ds(d * HALF, HALF)]).start()

    def add_up():
        far_block(1)
        image_side(FAR)
        image_finish()
        pay_copy(0).start()

    work = {
        0: lambda: far_block(0),
        1: add_up,
    }
    image_side(NEAR)
    for h in range(HOPS - 1):
        for k in range(CHUNKS):
            forward(1, h, k)
            slot = h * CHUNKS + k
            work.get(slot, lambda: None)()
            if slot in SUM_SLOTS:
                sum_step(SUM_SLOTS.index(slot))
            if slot in FAR_SLOTS:
                far_add(FAR_SLOTS.index(slot))
            sent(0, h, k)

    for k in range(CHUNKS):
        for d in range(2):
            hop(1, HOPS - 1, k, d, landed(1, HOPS - 1, k, d)).wait_recv()
        rows = pl.ds(k * CHUNK, CHUNK)
        txt_grad_ref[rows] += hops[1, HOPS - 1, k]
        slot = (HOPS - 1) * CHUNKS + k
        if slot in SUM_SLOTS:
            sum_step(SUM_SLOTS.index(slot))

    for k in range(CHUNKS):
        sent(0, HOPS - 1, k)
        for h in range(HOPS):
            sent(1, h, k)
        far_copy(0, k, txt_hbm, far_in).wait_send()
        far_copy(1, k, far_ret, far_back).wait_send()
    for step in range(len(SUM_BITS)):
        on_senders(step, lambda: pay_copy(step).wait_send())


def finish(
    img_ref, txt_ref, total_ref, img_out, txt_out, gi_out, gt_out, *rest
):
    sums_out, sems = rest[:3], rest[3]
    copies = [
        pltpu.make_async_copy(img_ref, img_out, sems.at[0]),
        pltpu.make_async_copy(txt_ref, txt_out, sems.at[1]),
    ]
    for copy in copies:
        copy.start()
    for i in range(TILES):
        cols = pl.ds(i * LANES, LANES)
        gi_out[cols] = total_ref[0, i, 0]
        gt_out[cols] = total_ref[1, i, 0]
    for out, line in zip(
        sums_out, (total_ref[0, TILES + 1], total_ref[1, TILES], total_ref[0, TILES])
    ):
        out[...] = jnp.sum(line, axis=-1, keepdims=True) / (
            3.0 * ROWS * ROWS * (1 << BITS)
        )
    for copy in copies:
        copy.wait()


def shards(
    picture_encoder_result,
    caption_encoder_result,
    picture_channel_factor,
    caption_channel_factor,
    logit_multiplier,
    logit_offset,
):
    f32 = jnp.float32
    vmem = pl.BlockSpec(memory_space=pltpu.VMEM)
    hbm = pl.BlockSpec(memory_space=pltpu.HBM)
    dma = pltpu.SemaphoreType.DMA
    wide = jax.ShapeDtypeStruct((ROWS, D), f32)
    image_grad, text_grad, total = pl.pallas_call(
        kernel,
        name="contrast",
        out_shape=(
            wide,
            wide,
            jax.ShapeDtypeStruct((2, PAY, 1, LANES), f32),
        ),
        in_specs=[hbm] * 6,
        out_specs=(vmem, vmem, vmem),
        scratch_shapes=[
            pltpu.SMEM((1,), f32),
            pltpu.SMEM((1,), f32),
            pltpu.VMEM((D,), f32),
            pltpu.VMEM((D,), f32),
            pltpu.VMEM((ROWS, D), f32),
            pltpu.VMEM((ROWS, D), f32),
            pltpu.VMEM((ROWS, D), f32),
            pltpu.VMEM((ROWS, D), f32),
            pltpu.VMEM((2, HOPS, CHUNKS, CHUNK, D), f32),
            pltpu.VMEM((CHUNKS, CHUNK, D), f32),
            pltpu.VMEM((ROWS, D), f32),
            pltpu.VMEM((ROWS, D), f32),
            pltpu.VMEM((ROWS, D), f32),
            pltpu.VMEM((3, ROWS, ROWS), f32),
            pltpu.VMEM((3, ROWS, D), f32),
            pltpu.VMEM((1, D), f32),
            pltpu.VMEM((8, LANES), f32),
            pltpu.VMEM((2, PAY, 1, LANES), f32),
            pltpu.VMEM((len(SUM_SLOTS) - 1, PAY, 1, LANES), f32),
            pltpu.VMEM((len(SUM_SLOTS) - 1, PAY, 1, LANES), f32),
            pltpu.SemaphoreType.REGULAR,
            pltpu.SemaphoreType.REGULAR,
            pltpu.SemaphoreType.REGULAR,
            dma((6,)),
            dma((2, HOPS, CHUNKS, 2)),
            dma((2, HOPS, CHUNKS, 2)),
            dma((2, CHUNKS)),
            dma((2, CHUNKS)),
            dma((len(SUM_SLOTS),)),
            dma((len(SUM_SLOTS),)),
        ],
        compiler_params=pltpu.CompilerParams(
            collective_id=0, has_side_effects=True, vmem_limit_bytes=51 << 20
        ),
        cost_estimate=pl.CostEstimate(
            flops=18 * ROWS * ROWS * D,
            bytes_accessed=16 * ROWS * D,
            transcendentals=6 * ROWS * ROWS,
        ),
    )(
        logit_multiplier.reshape(1),
        logit_offset.reshape(1),
        picture_encoder_result,
        caption_encoder_result,
        pltpu.with_memory_space_constraint(picture_channel_factor, pltpu.HBM),
        pltpu.with_memory_space_constraint(caption_channel_factor, pltpu.HBM),
    )
    one = jax.ShapeDtypeStruct((1, 1), f32)
    line = jax.ShapeDtypeStruct((D,), f32)
    *results, temp, bias, loss = pl.pallas_call(
        finish,
        name="results",
        out_shape=(wide, wide, line, line, one, one, one),
        in_specs=[vmem] * 3,
        out_specs=(hbm, hbm, vmem, vmem, vmem, vmem, vmem),
        scratch_shapes=[dma((2,))],
        compiler_params=pltpu.CompilerParams(vmem_limit_bytes=8 << 20),
    )(image_grad, text_grad, total)
    return (*results, temp[0, 0], bias[0, 0], loss[0, 0])


def solution(mesh):
    return jax.shard_map(
        shards,
        mesh=mesh,
        in_specs=(P("dp", None), P("dp", None), P(), P(), P(), P()),
        out_specs=(P("dp", None), P("dp", None), P(), P(), P(), P(), P()),
        check_vma=False,
    )
```

```python
import functools

import jax
import jax.numpy as jnp
from jax import lax
from jax.experimental import pallas as pl
from jax.experimental.pallas import tpu as pltpu
from jax.sharding import PartitionSpec as P

eps = 1e-06
MESH = pl.DeviceIdType.MESH

ROWS = 256
D = 1152
CHUNKS = 2
CHUNK = ROWS // CHUNKS
HALF = CHUNK // 2
Z = 16
HOPS = Z // 2
BITS = 9
FAR_BIT = 8
NEAR_BIT = 4
CROSS_BITS = (5, 6, 7, 8)
SUM_BITS = (0, 4, 1, 2, 3, 5, 6, 7, 8, 4, 0)
OVER, ACROSS = 1, len(SUM_BITS) - 2
SUM_SLOTS = (2, 4, 5, 6, 7, 8, 9, 10, 11, 13, 14)
FAR_SLOTS = (8, 12)
LANES = 128
TILES = D // LANES
PAY = TILES + 2
SELF, FAR, NEAR = 0, 1, 2


def flipped(me, bit):
    stride = 1 << bit
    return me + stride - 2 * stride * ((me // stride) % 2)


def z_shifted(me, step):
    z = (me // 2) % Z
    return me + 2 * ((z + step + Z) % Z - z)


def matmul(a, b, contract):
    return lax.dot_general(
        a,
        b,
        ((contract[:1], contract[1:]), ((), ())),
        precision=lax.Precision.HIGHEST,
        preferred_element_type=jnp.float32,
    )


def kernel(
    mult_hbm,
    offs_hbm,
    img_hbm,
    txt_hbm,
    gi_hbm,
    gt_hbm,
    img_grad_ref,
    txt_grad_ref,
    total_ref,
    mult_ref,
    offs_ref,
    gi_ref,
    gt_ref,
    img_raw,
    txt_raw,
    img_emb,
    d_img,
    hops,
    ret,
    far_in,
    far_ret,
    far_back,
    g_all,
    e_all,
    gain_acc,
    sum_acc,
    pay_all,
    pay,
    pay_in,
    ready,
    quarter,
    far_in_kernel,
    load_sem,
    send_sem,
    recv_sem,
    far_send,
    far_recv,
    pay_send,
    pay_recv,
):
    me = lax.axis_index("dp")
    core = me % 2
    mate = flipped(me, 0)
    ways = (z_shifted(me, 1), z_shifted(me, -1))
    far = flipped(me, FAR_BIT)

    def greet(sem, other):
        pl.semaphore_signal(sem, inc=1, device_id=(other,), device_id_type=MESH)

    place = (me // 2) % Z
    lower = place < HOPS
    upper = place >= HOPS
    barrier = pltpu.get_barrier_semaphore()
    for other in ways:
        greet(barrier, other - core * (1 - (other // 2) % Z // HOPS))

    @pl.when(upper)
    def _():
        greet(barrier, mate)
        pl.semaphore_wait(barrier, 3)

    @pl.when(lower)
    def _():
        for bit in CROSS_BITS:
            greet(barrier, flipped(me, bit) - core + 1)

    @pl.when(lower & (core == 1))
    def _():
        greet(barrier, mate)
        pl.semaphore_wait(ready, 1)

    @pl.when(lower & (core == 0))
    def _():
        pl.semaphore_wait(barrier, 5)
        greet(ready, mate)

    def meet_others():
        @pl.when(core == 1)
        def _():
            pl.semaphore_wait(barrier, 2 * len(CROSS_BITS))
            greet(ready, mate)

        @pl.when(core == 0)
        def _():
            pl.semaphore_wait(ready, 1)

    def at_ends(act):
        @pl.when(place == 0)
        def _():
            act(-1)

        @pl.when(place == HOPS - 1)
        def _():
            act(1)

    def quarter_in(_):
        greet(quarter, far)

    def tell_quarter(way):
        pl.semaphore_wait(quarter, 1)
        for i in range(1, HOPS // 2 + 1):
            greet(far_in_kernel, z_shifted(me, way * i))

    def hop(phase, h, k, d, src):
        return pltpu.make_async_remote_copy(
            src_ref=src,
            dst_ref=hops.at[phase, h, k, pl.ds(d * HALF, HALF)],
            send_sem=send_sem.at[phase, h, k, d],
            recv_sem=recv_sem.at[phase, h, k, d],
            device_id=(ways[d],),
            device_id_type=MESH,
        )

    def landed(phase, h, k, d):
        return hops.at[phase, h, k, pl.ds(d * HALF, HALF)]

    def forward(phase, h, k):
        for d in range(2):
            src = landed(phase, h, k, d)
            hop(phase, h, k, d, src).wait_recv()
            hop(phase, h + 1, k, d, src).start()

    def sent(phase, h, k):
        for d in range(2):
            hop(phase, h, k, d, landed(phase, h, k, d)).wait_send()

    def far_copy(leg, k, src, dst):
        return pltpu.make_async_remote_copy(
            src_ref=src.at[pl.ds(k * CHUNK, CHUNK)],
            dst_ref=dst.at[pl.ds(k * CHUNK, CHUNK)],
            send_sem=far_send.at[leg, k],
            recv_sem=far_recv.at[leg, k],
            device_id=(far,),
            device_id_type=MESH,
        )

    def pay_copy(step):
        first, last = step == 0, step == len(SUM_BITS) - 1
        return pltpu.make_async_remote_copy(
            src_ref=pay_all.at[1 - core] if first else pay.at[step - 1],
            dst_ref=total_ref.at[core] if last else pay_in.at[step],
            send_sem=pay_send.at[step],
            recv_sem=pay_recv.at[step],
            device_id=(flipped(me, SUM_BITS[step]),),
            device_id_type=MESH,
        )

    def on_senders(step, act):
        if step < OVER or step > ACROSS:
            act()
        else:
            pl.when(upper if step == OVER else lower)(act)

    def on_receivers(step, act):
        if step < OVER or step > ACROSS:
            act()
        else:
            pl.when(upper if step == ACROSS else lower)(act)

    def block(src, dst, pair, k):
        rows = pl.ds(k * CHUNK, CHUNK)
        feat = src[...]
        gain = gt_ref[...].reshape(1, D)
        scaled = feat * gain
        norm = jnp.sqrt(jnp.sum(scaled * scaled, axis=-1, keepdims=True) + eps)
        emb = scaled / norm
        e_all[pair, rows] = emb
        image = img_emb[...]
        dots = matmul(emb, image, (1, 1))
        logits = mult * dots + offs
        small = jnp.exp(-jnp.abs(logits))
        loss = jnp.maximum(logits, 0.0) + jnp.log1p(small)
        g = jnp.where(logits >= 0.0, 1.0, small) / (1.0 + small)
        if pair == SELF:
            text_row = k * CHUNK + lax.broadcasted_iota(jnp.int32, (CHUNK, ROWS), 0)
            image_row = lax.broadcasted_iota(jnp.int32, (CHUNK, ROWS), 1)
            labels = (text_row == image_row).astype(jnp.float32)
            loss = loss - labels * logits
            g = g - labels
        g_all[pair, rows] = g
        for i, term in enumerate((loss, g * dots, g)):
            line = jnp.sum(term, axis=0, keepdims=True)
            sum_acc[i : i + 1] += line[:, :LANES] + line[:, LANES:]
        d_emb = mult * matmul(g, image, (1, 0))
        d_scaled = (d_emb - emb * jnp.sum(emb * d_emb, axis=-1, keepdims=True)) / norm
        dst[...] = d_scaled * gain
        gain_acc[...] += jnp.sum(d_scaled * feat, axis=0, keepdims=True)

    def image_side(pair):
        for half in range(2):
            cols = pl.ds(half * CHUNK, CHUNK)
            part = mult * matmul(g_all[pair, :, cols], e_all[pair], (0, 0))
            if pair == SELF:
                d_img[cols] = part
            else:
                d_img[cols] += part

    def image_norm():
        for half in range(2):
            rows = pl.ds(half * CHUNK, CHUNK)
            scaled = img_raw[rows] * gi_ref[...].reshape(1, D)
            norm = jnp.sqrt(jnp.sum(scaled * scaled, axis=-1, keepdims=True) + eps)
            img_emb[rows] = scaled / norm

    def image_finish():
        total = jnp.zeros((1, D), jnp.float32)
        for half in range(2):
            rows = pl.ds(half * CHUNK, CHUNK)
            feat = img_raw[rows]
            gain = gi_ref[...].reshape(1, D)
            scaled = feat * gain
            norm = jnp.sqrt(jnp.sum(scaled * scaled, axis=-1, keepdims=True) + eps)
            emb = img_emb[rows]
            d_emb = d_img[rows]
            d_scaled = (
                d_emb - emb * jnp.sum(emb * d_emb, axis=-1, keepdims=True)
            ) / norm
            img_grad_ref[rows] = d_scaled * gain
            total = total + jnp.sum(d_scaled * feat, axis=0, keepdims=True)
        text = gain_acc[...]
        for i in range(TILES):
            pay_all[0, i] = total[:, i * LANES : (i + 1) * LANES]
            pay_all[1, i] = text[:, i * LANES : (i + 1) * LANES]
        pay_all[0, TILES] = sum_acc[0:1]
        pay_all[0, TILES + 1] = sum_acc[1:2]
        pay_all[1, TILES] = sum_acc[2:3]
        pay_all[1, TILES + 1] = jnp.zeros((1, LANES), jnp.float32)

    def sum_step(step):
        last = len(SUM_BITS) - 1

        def take():
            pay_copy(step).wait_recv()
            if step == 0:
                pay[0] = pay_all[core] + pay_in[0]
            elif step < ACROSS:
                pay[step] = pay[step - 1] + pay_in[step]
            elif step == ACROSS:
                pay[step] = pay_in[step]

        on_receivers(step, take)
        if step == ACROSS:

            @pl.when(lower)
            def _():
                pay[step] = pay[step - 1]

            total_ref[core] = pay[step]
        if step < last:
            on_senders(step + 1, lambda: pay_copy(step + 1).start())

    def self_block(k):
        rows = pl.ds(k * CHUNK, CHUNK)
        block(txt_raw.at[rows], txt_grad_ref.at[rows], SELF, k)

    def far_block(k):
        rows = pl.ds(k * CHUNK, CHUNK)
        far_copy(0, k, txt_hbm, far_in).wait_recv()
        block(far_in.at[rows], far_ret.at[rows], FAR, k)
        far_copy(1, k, far_ret, far_back).start()

    def far_add(k):
        rows = pl.ds(k * CHUNK, CHUNK)
        far_copy(1, k, far_ret, far_back).wait_recv()
        txt_grad_ref[rows] += far_back[rows]

    for k in range(CHUNKS):
        for d in range(2):
            hop(0, 0, k, d, txt_hbm.at[pl.ds(k * CHUNK + d * HALF, HALF)]).start()
    loads = [
        pltpu.make_async_copy(src, dst, load_sem.at[i])
        for i, (src, dst) in enumerate(
            (
                (mult_hbm, mult_ref),
                (offs_hbm, offs_ref),
                (gi_hbm, gi_ref),
                (gt_hbm, gt_ref),
                (img_hbm, img_raw),
                (txt_hbm, txt_raw),
            )
        )
    ]
    for load in loads:
        load.start()
    gain_acc[...] = jnp.zeros_like(gain_acc)
    sum_acc[...] = jnp.zeros_like(sum_acc)
    for load in loads:
        load.wait()
    mult = mult_ref[0]
    offs = offs_ref[0]
    image_norm()

    def far_start():
        for k in range(CHUNKS):
            far_copy(0, k, txt_hbm, far_in).start()

    def lower_start():
        @pl.when(lower)
        def _():
            meet_others()
            far_start()

    def upper_start():
        @pl.when(upper)
        def _():
            pl.semaphore_wait(far_in_kernel, 1)
            far_start()

    work = {
        0: lambda: self_block(0),
        1: lambda: self_block(1),
        2: lower_start,
        3: lambda: image_side(SELF),
        HOPS - 1: lambda: at_ends(quarter_in),
        HOPS: lambda: at_ends(tell_quarter),
        HOPS + 2: upper_start,
    }
    for h in range(HOPS - 1):
        for k in range(CHUNKS):
            forward(0, h, k)
            work.get(h * CHUNKS + k, lambda: None)()

    for k in range(CHUNKS):
        for d in range(2):
            hop(0, HOPS - 1, k, d, landed(0, HOPS - 1, k, d)).wait_recv()
        block(hops.at[0, HOPS - 1, k], ret.at[k], NEAR, k)
        for d in range(2):
            hop(1, 0, k, d, ret.at[k, pl.ds(d * HALF, HALF)]).start()

    def add_up():
        far_block(1)
        image_side(FAR)
        image_finish()
        pay_copy(0).start()

    work = {
        0: lambda: far_block(0),
        1: add_up,
    }
    image_side(NEAR)
    for h in range(HOPS - 1):
        for k in range(CHUNKS):
            forward(1, h, k)
            slot = h * CHUNKS + k
            work.get(slot, lambda: None)()
            if slot in SUM_SLOTS:
                sum_step(SUM_SLOTS.index(slot))
            if slot in FAR_SLOTS:
                far_add(FAR_SLOTS.index(slot))
            sent(0, h, k)

    for k in range(CHUNKS):
        for d in range(2):
            hop(1, HOPS - 1, k, d, landed(1, HOPS - 1, k, d)).wait_recv()
        rows = pl.ds(k * CHUNK, CHUNK)
        txt_grad_ref[rows] += hops[1, HOPS - 1, k]
        slot = (HOPS - 1) * CHUNKS + k
        if slot in SUM_SLOTS:
            sum_step(SUM_SLOTS.index(slot))

    for k in range(CHUNKS):
        sent(0, HOPS - 1, k)
        for h in range(HOPS):
            sent(1, h, k)
        far_copy(0, k, txt_hbm, far_in).wait_send()
        far_copy(1, k, far_ret, far_back).wait_send()
    for step in range(len(SUM_BITS)):
        on_senders(step, lambda: pay_copy(step).wait_send())


def finish(
    img_ref, txt_ref, total_ref, img_out, txt_out, gi_out, gt_out, *rest
):
    sums_out, sems = rest[:3], rest[3]
    copies = [
        pltpu.make_async_copy(img_ref, img_out, sems.at[0]),
        pltpu.make_async_copy(txt_ref, txt_out, sems.at[1]),
    ]
    for copy in copies:
        copy.start()
    for i in range(TILES):
        cols = pl.ds(i * LANES, LANES)
        gi_out[cols] = total_ref[0, i, 0]
        gt_out[cols] = total_ref[1, i, 0]
    for out, line in zip(
        sums_out, (total_ref[0, TILES + 1], total_ref[1, TILES], total_ref[0, TILES])
    ):
        out[...] = jnp.sum(line, axis=-1, keepdims=True) / (
            3.0 * ROWS * ROWS * (1 << BITS)
        )
    for copy in copies:
        copy.wait()


def shards(
    picture_encoder_result,
    caption_encoder_result,
    picture_channel_factor,
    caption_channel_factor,
    logit_multiplier,
    logit_offset,
):
    f32 = jnp.float32
    vmem = pl.BlockSpec(memory_space=pltpu.VMEM)
    hbm = pl.BlockSpec(memory_space=pltpu.HBM)
    dma = pltpu.SemaphoreType.DMA
    wide = jax.ShapeDtypeStruct((ROWS, D), f32)
    image_grad, text_grad, total = pl.pallas_call(
        kernel,
        name="contrast",
        out_shape=(
            wide,
            wide,
            jax.ShapeDtypeStruct((2, PAY, 1, LANES), f32),
        ),
        in_specs=[hbm] * 6,
        out_specs=(vmem, vmem, vmem),
        scratch_shapes=[
            pltpu.SMEM((1,), f32),
            pltpu.SMEM((1,), f32),
            pltpu.VMEM((D,), f32),
            pltpu.VMEM((D,), f32),
            pltpu.VMEM((ROWS, D), f32),
            pltpu.VMEM((ROWS, D), f32),
            pltpu.VMEM((ROWS, D), f32),
            pltpu.VMEM((ROWS, D), f32),
            pltpu.VMEM((2, HOPS, CHUNKS, CHUNK, D), f32),
            pltpu.VMEM((CHUNKS, CHUNK, D), f32),
            pltpu.VMEM((ROWS, D), f32),
            pltpu.VMEM((ROWS, D), f32),
            pltpu.VMEM((ROWS, D), f32),
            pltpu.VMEM((3, ROWS, ROWS), f32),
            pltpu.VMEM((3, ROWS, D), f32),
            pltpu.VMEM((1, D), f32),
            pltpu.VMEM((8, LANES), f32),
            pltpu.VMEM((2, PAY, 1, LANES), f32),
            pltpu.VMEM((len(SUM_SLOTS) - 1, PAY, 1, LANES), f32),
            pltpu.VMEM((len(SUM_SLOTS) - 1, PAY, 1, LANES), f32),
            pltpu.SemaphoreType.REGULAR,
            pltpu.SemaphoreType.REGULAR,
            pltpu.SemaphoreType.REGULAR,
            dma((6,)),
            dma((2, HOPS, CHUNKS, 2)),
            dma((2, HOPS, CHUNKS, 2)),
            dma((2, CHUNKS)),
            dma((2, CHUNKS)),
            dma((len(SUM_SLOTS),)),
            dma((len(SUM_SLOTS),)),
        ],
        compiler_params=pltpu.CompilerParams(
            collective_id=0, has_side_effects=True, vmem_limit_bytes=51 << 20
        ),
        cost_estimate=pl.CostEstimate(
            flops=18 * ROWS * ROWS * D,
            bytes_accessed=16 * ROWS * D,
            transcendentals=6 * ROWS * ROWS,
        ),
    )(
        logit_multiplier.reshape(1),
        logit_offset.reshape(1),
        picture_encoder_result,
        caption_encoder_result,
        pltpu.with_memory_space_constraint(picture_channel_factor, pltpu.HBM),
        pltpu.with_memory_space_constraint(caption_channel_factor, pltpu.HBM),
    )
    one = jax.ShapeDtypeStruct((1, 1), f32)
    line = jax.ShapeDtypeStruct((D,), f32)
    *results, temp, bias, loss = pl.pallas_call(
        finish,
        name="results",
        out_shape=(wide, wide, line, line, one, one, one),
        in_specs=[vmem] * 3,
        out_specs=(hbm, hbm, vmem, vmem, vmem, vmem, vmem),
        scratch_shapes=[dma((2,))],
        compiler_params=pltpu.CompilerParams(vmem_limit_bytes=8 << 20),
    )(image_grad, text_grad, total)
    return (*results, temp[0, 0], bias[0, 0], loss[0, 0])


def solution(mesh):
    return jax.shard_map(
        shards,
        mesh=mesh,
        in_specs=(P("dp", None), P("dp", None), P(), P(), P(), P()),
        out_specs=(P("dp", None), P("dp", None), P(), P(), P(), P(), P()),
        check_vma=False,
    )
```
